32 devices in a mesh: ax: 2 (over x), az: 4 (over z), rad: 4 (over y, core).
Axes of the slice: x: 2, y: 2, z: 4, core: 2. Of those that a mesh axis runs over, the one named last changes fastest.
Arguments:
- velocity: float32 [512, 64, 512], P('rad', 'az', 'ax'), may hold values from -4 to 4
- radial_courant: bfloat16 [512, 64, 512], P('rad', 'az', 'ax'), may hold values from -0.5 to 0.5
- axial_courant: bfloat16 [512, 64, 512], P('rad', 'az', 'ax'), may hold values from -0.5 to 0.5
- radial_diffusion: float32 [512], P('rad'), may hold values from 2048 to 8192
Outputs:
- advanced: float32 [512, 64, 512], P('rad', 'az', 'ax')
The draws below stay inside these ranges and needn't reach their ends.
All inputs are finite; a program needn't handle non-finite values.
Results may differ from the reference program's by a relative error of at most 0.0009.
Values sent between devices are 32-bit elements; how exact they have to be, the bound alone decides.
A program may use at most 64 MiB of HBM per device.

```python
import math
import jax
import jax.numpy as jnp
from jax import lax

NR = 512
STEPS = 6
NT = 64
NZ = 512


def levels(stream_key, extent, split, smallest, largest):
    level, own = 1.0, jax.random.fold_in(stream_key, 6)
    for axis_at, blocks in split:
        steps = jnp.exp(jax.random.uniform(jax.random.fold_in(own, axis_at), (blocks,), jnp.float32, smallest / len(split), largest / len(split)))
        level = level * jnp.repeat(steps, extent[axis_at] // blocks).reshape([-1 if axis == axis_at else 1 for axis in range(len(extent))])
    return level


def noise(stream_key, shape, scale, limit, shards=(), held_as=jnp.bfloat16):
    result = scale * jax.random.normal(stream_key, shape, jnp.float32)
    if shards:
        result = result * levels(stream_key, shape, shards, -0.22, 0.18)
    return jnp.clip(result, -limit, limit).astype(held_as)


def setup_inputs(seed: int = 0) -> dict:
    keys = jax.random.split(jax.random.key(seed), 5)
    return {
        "velocity": noise(keys[0], (NR, NT, NZ), 1.0, 4.0, ((0, 4), (1, 4), (2, 2)), jnp.float32),
        "radial_courant": jnp.clip(jax.random.uniform(keys[1], (NR, NT, NZ), jnp.float32, -0.5, 0.5) * levels(keys[1], (NR, NT, NZ), ((0, 4), (1, 4), (2, 2)), -0.4, 0.0), -0.5, 0.5).astype(jnp.bfloat16),
        "axial_courant": jnp.clip(jax.random.uniform(keys[2], (NR, NT, NZ), jnp.float32, -0.5, 0.5) * levels(keys[2], (NR, NT, NZ), ((0, 4), (1, 4), (2, 2)), -0.4, 0.0), -0.5, 0.5).astype(jnp.bfloat16),
        "radial_diffusion": jnp.clip(jnp.exp(math.log(8192.0) - 1.3862944 * jax.random.uniform(keys[3], (NR,), jnp.float32) ** levels(keys[3], (NR,), ((0, 4),), -0.2, 0.2)), 2048.0, 8192.0),
    }


theta_rate = 0.25
axial_mixing = 0.25
azimuth_mixing = 0.25

def radial_terms(radial_diffusion, position):
    spacing = 1.0 / (NR + 1)
    radius = 1.0 + (position + 1.0) * spacing
    inward = radial_diffusion * (radius - 0.5 * spacing) / radius
    outward = radial_diffusion * (radius + 0.5 * spacing) / radius
    curvature = radial_diffusion * spacing * spacing / (radius * radius)
    return (radius, inward, outward, curvature)

def right_side(state_field, radial_lower, radial_upper, axial_minus_two, axial_minus_one, axial_plus_one, axial_plus_two, azimuth_minus_two, azimuth_minus_one, azimuth_plus_one, azimuth_plus_two, radial_courant, axial_courant, radius, inward, outward, curvature):
    radius_col = radius[:, None, None]
    spread = outward[:, None, None] * (radial_upper - state_field) - inward[:, None, None] * (state_field - radial_lower) - curvature[:, None, None] * state_field
    radial_slope = 0.5 * (radial_upper - radial_lower)
    axial_slope = (8.0 * (axial_plus_one - axial_minus_one) - (axial_plus_two - axial_minus_two)) / 12.0
    axial_curve = (16.0 * (axial_plus_one + axial_minus_one) - (axial_plus_two + axial_minus_two) - 30.0 * state_field) / 12.0
    azimuth_slope = (8.0 * (azimuth_plus_one - azimuth_minus_one) - (azimuth_plus_two - azimuth_minus_two)) / 12.0
    azimuth_curve = (16.0 * (azimuth_plus_one + azimuth_minus_one) - (azimuth_plus_two + azimuth_minus_two) - 30.0 * state_field) / 12.0
    transport = radial_courant * radial_slope + axial_courant * axial_slope + theta_rate * state_field * azimuth_slope / radius_col
    mixing = axial_mixing * axial_curve + azimuth_mixing * azimuth_curve / (radius_col * radius_col)
    return state_field + spread - transport + mixing

def reference(velocity, radial_courant, axial_courant, radial_diffusion):
    position = jnp.arange(NR).astype(radial_diffusion.dtype)
    radius, inward, outward, curvature = radial_terms(radial_diffusion, position)
    zero_one = jnp.zeros((1,), radial_diffusion.dtype)
    lower_diag = jnp.concatenate([zero_one, -inward[1:]])
    upper_diag = jnp.concatenate([-outward[:-1], zero_one])
    main_diag = 1.0 + inward + outward + curvature
    state_field = velocity
    for turn_index in range(STEPS):
        padded_radial = jnp.pad(state_field, ((1, 1), (0, 0), (0, 0)))
        padded_axial = jnp.pad(state_field, ((0, 0), (0, 0), (2, 2)))
        right_hand = right_side(state_field, padded_radial[:-2], padded_radial[2:], padded_axial[:, :, :-4], padded_axial[:, :, 1:-3], padded_axial[:, :, 3:-1], padded_axial[:, :, 4:], jnp.roll(state_field, 2, axis=1), jnp.roll(state_field, 1, axis=1), jnp.roll(state_field, -1, axis=1), jnp.roll(state_field, -2, axis=1), radial_courant, axial_courant, radius, inward, outward, curvature)
        solved = lax.linalg.tridiagonal_solve(lower_diag, main_diag, upper_diag, right_hand.reshape(NR, -1))
        state_field = solved.reshape(state_field.shape)
    return state_field
```

```python
import functools

import jax
import jax.numpy as jnp
from jax import lax
from jax.experimental import pallas as pl
from jax.experimental.pallas import tpu as pltpu
from jax.sharding import PartitionSpec as P

NR = 512
STEPS = 6
F32 = jnp.float32
MESH = pl.DeviceIdType.MESH
PAD = 8
CH = 32


def join_slabs(left, right):
    head_l, tail_l, tl = left
    head_r, tail_r, tr = right
    divisor = 1.0 - tl[3] * tr[0]
    mid_value = (tail_l - tl[3] * head_r) / divisor
    mid_left = tl[2] / divisor
    mid_right = -tl[3] * tr[1] / divisor
    next_value = head_r - tr[0] * mid_value
    next_left = -tr[0] * mid_left
    next_right = tr[1] - tr[0] * mid_right
    return (
        head_l - tl[1] * next_value,
        tail_r - tr[2] * mid_value,
        (
            tl[0] - tl[1] * next_left,
            -tl[1] * next_right,
            -tr[2] * mid_left,
            tr[3] - tr[2] * mid_right,
        ),
    )


def interface_rows(members, me, n):
    zero = jnp.zeros_like(members[0][0])
    identity = (zero, zero, (zero, zero - 1.0, zero - 1.0, zero))

    def choose(cond, a, b):
        return jax.tree.map(lambda x, y: jnp.where(cond, x, y), a, b)

    prefix = identity
    own = members[0]
    for k in range(n):
        own = choose(k == me, members[k], own)
        prefix = choose(k < me, join_slabs(prefix, members[k]), prefix)
    suffix = identity
    for k in range(n - 1, -1, -1):
        suffix = choose(k > me, join_slabs(members[k], suffix), suffix)
    combined = join_slabs(own, suffix)
    lower = (prefix[1] - prefix[2][3] * combined[0]) / (1.0 - prefix[2][3] * combined[2][0])
    upper = (suffix[0] - suffix[2][0] * (own[1] - own[2][2] * lower)) / (
        1.0 - suffix[2][0] * own[2][3]
    )
    return lower, upper


def kernel(
    n, naz, R, NTL, NZL,
    v, rc, ac, kc, out,
    F, Y, Q, HA, PS, PR, RB0, RBE, RBI, TB, MI, CP, SPK, CF, LU,
    az_ss, az_rs, ax_ss, ax_rs, r0_ss, r0_rs, re_ss, re_rs, ri_ss, ri_rs, t_ss, t_rs,
):
    me = lax.axis_index("rad")
    az = lax.axis_index("az")
    ax = lax.axis_index("ax")
    left = lax.rem(az + naz - 1, naz)
    right = lax.rem(az + 1, naz)
    other = 1 - ax
    peers = [lax.rem(me + d, n) for d in range(1, n)]
    NI = NTL - 4

    barrier = pltpu.get_barrier_semaphore()
    for p in peers:
        pl.semaphore_signal(barrier, inc=1, device_id={"rad": p}, device_id_type=MESH)
    for p in (left, right):
        pl.semaphore_signal(barrier, inc=1, device_id={"az": p}, device_id_type=MESH)
    pl.semaphore_signal(barrier, inc=1, device_id={"ax": other}, device_id_type=MESH)
    pl.semaphore_wait(barrier, n + 2)

    def az_copy(s, side):
        if side == 0:
            src, dst, to = F.at[pl.ds(2, 2), pl.ds(PAD, R)], HA.at[s, 1], left
        else:
            src, dst, to = F.at[pl.ds(NTL, 2), pl.ds(PAD, R)], HA.at[s, 0], right
        return pltpu.make_async_remote_copy(
            src_ref=src, dst_ref=dst, send_sem=az_ss.at[s, side],
            recv_sem=az_rs.at[s, 1 - side], device_id={"az": to}, device_id_type=MESH)

    def ax_copy(s):
        return pltpu.make_async_remote_copy(
            src_ref=PS.at[s], dst_ref=PR.at[s], send_sem=ax_ss.at[s],
            recv_sem=ax_rs.at[s], device_id={"ax": other}, device_id_type=MESH)

    def rad_send(buf, ss, rs, d):
        return pltpu.make_async_remote_copy(
            src_ref=buf.at[me], dst_ref=buf.at[me], send_sem=ss.at[d],
            recv_sem=rs.at[me], device_id={"rad": peers[d]}, device_id_type=MESH)

    def rad_recv(buf, ss, rs, d):
        return pltpu.make_async_remote_copy(
            src_ref=buf.at[me], dst_ref=buf.at[peers[d]], send_sem=ss.at[d],
            recv_sem=rs.at[peers[d]], device_id={"rad": peers[d]}, device_id_type=MESH)

    lane = lax.broadcasted_iota(jnp.int32, (CH, 128), 1)

    def pack(s):
        def body(c, carry):
            r0 = pl.multiple_of(c * CH, CH)

            def one(j, acc):
                edge = jnp.where(
                    ax == 0,
                    F[j + 2, pl.ds(PAD + r0, CH), pl.ds(NZL - 128, 128)],
                    F[j + 2, pl.ds(PAD + r0, CH), pl.ds(0, 128)],
                )
                moved = pltpu.roll(edge, 2 * j + 2 * (1 - ax), 1)
                return jnp.where(lane // 2 == j, moved, acc)

            PS[s, pl.ds(r0, CH), :] = lax.fori_loop(0, NTL, one, jnp.zeros((CH, 128), F32))
            return carry

        lax.fori_loop(0, R // CH, body, 0)

    def fill(j, carry):
        F[j + 2, pl.ds(PAD, R), :] = v[j]
        RB0[me, pl.ds(j, 1), :] = v[j, 0:1, :]
        RB0[me, pl.ds(NTL + j, 1), :] = v[j, R - 1 : R, :]
        return carry

    lax.fori_loop(0, NTL, fill, 0)
    az_copy(0, 0).start()
    az_copy(0, 1).start()
    for d in range(n - 1):
        rad_send(RB0, r0_ss, r0_rs, d).start()
    pack(0)
    ax_copy(0).start()

    lane1 = lax.broadcasted_iota(jnp.int32, (1, 128), 1)

    def forward(i, carry):
        delta, row = carry
        inw = kc[0, pl.ds(i, 1), :]
        outw = kc[1, pl.ds(i, 1), :]
        t = 1.0 + kc[2, pl.ds(i, 1), :] + inw * delta
        inv = 1.0 / (outw + t)
        unit = jnp.where(lane1 == i, 1.0, 0.0)
        row = (unit + inw * row) * inv
        MI[pl.ds(i, 1), :] = row
        CP[pl.ds(i, 1), :] = outw * inv
        return t * inv, row

    lax.fori_loop(0, R, forward, (jnp.ones((1, 128), F32), jnp.zeros((1, 128), F32)))

    def backward(t, row):
        i = R - 2 - t
        row = MI[pl.ds(i, 1), :] + CP[pl.ds(i, 1), :] * row
        MI[pl.ds(i, 1), :] = row
        return row

    lax.fori_loop(0, R - 1, backward, MI[R - 1 : R, :])
    SPK[0] = -kc[0, 0:1, :] * jnp.broadcast_to(MI[:, 0:1], (R, 128))
    SPK[1] = -kc[1, R - 1 : R, :] * jnp.broadcast_to(MI[:, R - 1 : R], (R, 128))
    TB[me, 0:1, :] = SPK[0, 0:1, :]
    TB[me, 1:2, :] = SPK[1, 0:1, :]
    TB[me, 2:3, :] = SPK[0, R - 1 : R, :]
    TB[me, 3:4, :] = SPK[1, R - 1 : R, :]
    TB[me, 4:8, :] = jnp.zeros((4, 128), F32)
    for d in range(n - 1):
        rad_send(TB, t_ss, t_rs, d).start()

    for d in range(n - 1):
        rad_recv(RB0, r0_ss, r0_rs, d).wait_recv()
    below = jnp.maximum(me - 1, 0)
    above = jnp.minimum(me + 1, n - 1)
    LU[0] = jnp.where(me > 0, RB0[below, NTL : 2 * NTL, :], 0.0)
    LU[1] = jnp.where(me < n - 1, RB0[above, 0:NTL, :], 0.0)

    def halo_rows(j, carry):
        F[j + 2, PAD - 1 : PAD, :] = LU[0, pl.ds(j, 1), :]
        F[j + 2, PAD + R : PAD + R + 1, :] = LU[1, pl.ds(j, 1), :]
        return carry

    lax.fori_loop(0, NTL, halo_rows, 0)

    for d in range(n - 1):
        rad_recv(TB, t_ss, t_rs, d).wait_recv()
    members = []
    for k in range(n):
        members.append((
            jnp.where(lane1 == k, 1.0, 0.0),
            jnp.where(lane1 == n + k, 1.0, 0.0),
            tuple(TB[k, q : q + 1, :] for q in range(4)),
        ))
    lower_map, upper_map = interface_rows(members, me, n)
    for m in range(2 * n):
        for h, vec in enumerate((lower_map, upper_map)):
            val = jnp.sum(jnp.where(lane1 == m, vec, 0.0), axis=1, keepdims=True)
            CF[h, m : m + 1, :] = jnp.broadcast_to(val, (1, NZL))

    ml = jnp.where(ax == 1, 1.0, 0.0).astype(F32)
    mr = jnp.where(ax == 0, 1.0, 0.0).astype(F32)

    def wide(x):
        return jnp.concatenate([x] * (NZL // 128), axis=1)

    def solve_one(s, j):
        for c in range(R // CH):
            r0 = c * CH
            rows = pl.ds(PAD + r0, CH)
            f = F[j + 2, rows, :]
            m1, m2 = F[j + 1, rows, :], F[j, rows, :]
            p1, p2 = F[j + 3, rows, :], F[j + 4, rows, :]
            lo = F[j + 2, pl.ds(PAD + r0 - 1, CH), :]
            up = F[j + 2, pl.ds(PAD + r0 + 1, CH), :]
            ct = wide(kc[3, pl.ds(r0, CH), :])
            cl = wide(kc[4, pl.ds(r0, CH), :])
            halo = pltpu.roll(PR[s, pl.ds(r0, CH), :], 128 - 2 * j, 1)
            halo1 = pltpu.roll(halo, 127, 1)
            halo2 = pltpu.roll(halo, 126, 1)
            tiles = [f[:, i * 128 : (i + 1) * 128] for i in range(NZL // 128)]
            shifted = {}
            for k in (1, 2):
                down = [pltpu.roll(t, k, 1) for t in tiles]
                edge = ml * (halo1 if k == 1 else halo)
                shifted[-k] = jnp.concatenate([
                    jnp.where(lane < k, edge if i == 0 else down[i - 1], down[i])
                    for i in range(len(tiles))], axis=1)
                rise = [pltpu.roll(t, 128 - k, 1) for t in tiles]
                edge = mr * (halo1 if k == 1 else halo2)
                shifted[k] = jnp.concatenate([
                    jnp.where(lane >= 128 - k,
                              edge if i == len(tiles) - 1 else rise[i + 1], rise[i])
                    for i in range(len(tiles))], axis=1)
            z1d = shifted[1] - shifted[-1]
            z2d = shifted[2] - shifted[-2]
            z1s = shifted[1] + shifted[-1]
            z2s = shifted[2] + shifted[-2]
            rcv = rc[j, pl.ds(r0, CH), :].astype(F32)
            acv = ac[j, pl.ds(r0, CH), :].astype(F32)
            f30 = 30.0 * f
            q = (
                2.0 * f
                - (0.5 * rcv) * (up - lo)
                - (acv * (1.0 / 12.0)) * (8.0 * z1d - z2d)
                + (0.25 / 12.0) * (16.0 * z1s - z2s - f30)
                + ct * f * (8.0 * (p1 - m1) - (p2 - m2))
                + cl * (16.0 * (p1 + m1) - (p2 + m2) - f30)
            )
            Q[pl.ds(r0, CH), :] = q
        y = jnp.dot(MI[:, 0:R], Q[...], precision=lax.Precision.HIGHEST,
                    preferred_element_type=F32)
        Y[j] = y
        return y[0:1, :], y[R - 1 : R, :]

    def edge_of(e):
        return e + (NTL - 4) * (e // 2)

    def finish(s, j):
        low = LU[0, pl.ds(j, 1), :]
        high = LU[1, pl.ds(j, 1), :]
        for c in range(R // CH):
            rows = pl.ds(PAD + c * CH, CH)
            x = (
                Y[j, pl.ds(c * CH, CH), :]
                - wide(SPK[0, pl.ds(c * CH, CH), :]) * low
                - wide(SPK[1, pl.ds(c * CH, CH), :]) * high
                - F[j + 2, rows, :]
            )
            F[j + 2, rows, :] = x
            out[j, pl.ds(c * CH, CH), :] = x
        F[j + 2, PAD - 1 : PAD, :] = low - F[j + 2, PAD - 1 : PAD, :]
        F[j + 2, PAD + R : PAD + R + 1, :] = high - F[j + 2, PAD + R : PAD + R + 1, :]

    def ends(buf, s, half):
        res = []
        for h in range(2):
            total = None
            for k in range(n):
                for w in range(2):
                    term = (CF[h, w * n + k : w * n + k + 1, :]
                            * buf[s, k, w * half : (w + 1) * half, :])
                    total = term if total is None else total + term
            res.append(total)
        return res

    def step(s, carry):
        ax_copy(s).wait_recv()

        def inner(jj, c):
            first, last = solve_one(s, jj + 2)
            RBI[s, me, pl.ds(jj, 1), :] = first
            RBI[s, me, pl.ds(NI + jj, 1), :] = last
            return c

        lax.fori_loop(0, NI, inner, 0)
        for d in range(n - 1):
            rad_send(RBI.at[s], ri_ss.at[s], ri_rs.at[s], d).start()
        for side in range(2):
            az_copy(s, side).wait_recv()
        for i in range(2):
            F[i, pl.ds(PAD, R), :] = HA[s, 0, i]
            F[NTL + 2 + i, pl.ds(PAD, R), :] = HA[s, 1, i]

        def outer(e, c):
            first, last = solve_one(s, edge_of(e))
            RBE[s, me, pl.ds(e, 1), :] = first
            RBE[s, me, pl.ds(4 + e, 1), :] = last
            return c

        lax.fori_loop(0, 4, outer, 0)
        for d in range(n - 1):
            rad_send(RBE.at[s], re_ss.at[s], re_rs.at[s], d).start()
        for side in range(2):
            az_copy(s, side).wait_send()
        for d in range(n - 1):
            rad_recv(RBE.at[s], re_ss.at[s], re_rs.at[s], d).wait_recv()
        for h, rows in enumerate(ends(RBE, s, 4)):
            LU[h, 0:2, :] = rows[0:2]
            LU[h, NTL - 2 : NTL, :] = rows[2:4]

        def outer2(e, c):
            finish(s, edge_of(e))
            return c

        lax.fori_loop(0, 4, outer2, 0)

        @pl.when(s < STEPS - 1)
        def _():
            az_copy(s + 1, 0).start()
            az_copy(s + 1, 1).start()

        for d in range(n - 1):
            rad_recv(RBI.at[s], ri_ss.at[s], ri_rs.at[s], d).wait_recv()
        for h, rows in enumerate(ends(RBI, s, NI)):
            LU[h, 2 : NTL - 2, :] = rows

        def inner2(jj, c):
            finish(s, jj + 2)
            return c

        lax.fori_loop(0, NI, inner2, 0)

        @pl.when(s < STEPS - 1)
        def _():
            pack(s + 1)
            ax_copy(s + 1).start()

        ax_copy(s).wait_send()
        for d in range(n - 1):
            rad_send(RBE.at[s], re_ss.at[s], re_rs.at[s], d).wait_send()
            rad_send(RBI.at[s], ri_ss.at[s], ri_rs.at[s], d).wait_send()
        return carry

    lax.fori_loop(0, STEPS, step, 0)
    for d in range(n - 1):
        rad_send(RB0, r0_ss, r0_rs, d).wait_send()
        rad_send(TB, t_ss, t_rs, d).wait_send()


def local(n, naz, velocity, radial_courant, axial_courant, radial_diffusion):
    R, NTL, NZL = velocity.shape
    position = (lax.axis_index("rad") * R).astype(F32) + jnp.arange(R).astype(F32)
    spacing = 1.0 / (NR + 1)
    radius = 1.0 + (position + 1.0) * spacing
    inward = radial_diffusion * (radius - 0.5 * spacing) / radius
    outward = radial_diffusion * (radius + 0.5 * spacing) / radius
    sink = radial_diffusion * spacing * spacing / (radius * radius)
    kc = jnp.stack([inward, outward, sink, -(0.25 / 12.0) / radius,
                    (0.25 / 12.0) / (radius * radius)])
    kc = jnp.broadcast_to(kc[:, :, None], (5, R, 128))
    turn = lambda a: jnp.transpose(a, (1, 0, 2))
    S = STEPS
    dma = pltpu.SemaphoreType.DMA
    res = pl.pallas_call(
        functools.partial(kernel, n, naz, R, NTL, NZL),
        out_shape=jax.ShapeDtypeStruct((NTL, R, NZL), F32),
        in_specs=[pl.BlockSpec(memory_space=pltpu.VMEM)] * 4,
        out_specs=pl.BlockSpec(memory_space=pltpu.VMEM),
        scratch_shapes=[
            pltpu.VMEM((NTL + 4, R + 2 * PAD, NZL), F32),
            pltpu.VMEM((NTL, R, NZL), F32),
            pltpu.VMEM((R, NZL), F32),
            pltpu.VMEM((S, 2, 2, R, NZL), F32),
            pltpu.VMEM((S, R, 128), F32),
            pltpu.VMEM((S, R, 128), F32),
            pltpu.VMEM((n, 2 * NTL, NZL), F32),
            pltpu.VMEM((S, n, 8, NZL), F32),
            pltpu.VMEM((S, n, 2 * (NTL - 4), NZL), F32),
            pltpu.VMEM((n, 8, 128), F32),
            pltpu.VMEM((R, 128), F32),
            pltpu.VMEM((R, 128), F32),
            pltpu.VMEM((2, R, 128), F32),
            pltpu.VMEM((2, 2 * n, NZL), F32),
            pltpu.VMEM((2, NTL, NZL), F32),
            dma((S, 2)), dma((S, 2)), dma((S,)), dma((S,)),
            dma((n,)), dma((n,)), dma((S, n)), dma((S, n)),
            dma((S, n)), dma((S, n)), dma((n,)), dma((n,)),
        ],
        compiler_params=pltpu.CompilerParams(
            collective_id=0, has_side_effects=True, vmem_limit_bytes=48 * 1024 * 1024),
    )(turn(velocity), turn(radial_courant), turn(axial_courant), kc)
    return turn(res)


def solution(mesh):
    return jax.shard_map(
        functools.partial(local, mesh.shape["rad"], mesh.shape["az"]),
        mesh=mesh,
        in_specs=(P("rad", "az", "ax"), P("rad", "az", "ax"), P("rad", "az", "ax"), P("rad")),
        out_specs=P("rad", "az", "ax"),
        check_vma=False,
    )
```

```python
import functools

import jax
import jax.numpy as jnp
from jax import lax
from jax.experimental import pallas as pl
from jax.experimental.pallas import tpu as pltpu
from jax.sharding import PartitionSpec as P

NR = 512
STEPS = 6
F32 = jnp.float32
MESH = pl.DeviceIdType.MESH
PAD = 8
CH = 32


def join_slabs(left, right):
    head_l, tail_l, tl = left
    head_r, tail_r, tr = right
    divisor = 1.0 - tl[3] * tr[0]
    mid_value = (tail_l - tl[3] * head_r) / divisor
    mid_left = tl[2] / divisor
    mid_right = -tl[3] * tr[1] / divisor
    next_value = head_r - tr[0] * mid_value
    next_left = -tr[0] * mid_left
    next_right = tr[1] - tr[0] * mid_right
    return (
        head_l - tl[1] * next_value,
        tail_r - tr[2] * mid_value,
        (
            tl[0] - tl[1] * next_left,
            -tl[1] * next_right,
            -tr[2] * mid_left,
            tr[3] - tr[2] * mid_right,
        ),
    )


def interface_rows(members, me, n):
    zero = jnp.zeros_like(members[0][0])
    identity = (zero, zero, (zero, zero - 1.0, zero - 1.0, zero))

    def choose(cond, a, b):
        return jax.tree.map(lambda x, y: jnp.where(cond, x, y), a, b)

    prefix = identity
    own = members[0]
    for k in range(n):
        own = choose(k == me, members[k], own)
        prefix = choose(k < me, join_slabs(prefix, members[k]), prefix)
    suffix = identity
    for k in range(n - 1, -1, -1):
        suffix = choose(k > me, join_slabs(members[k], suffix), suffix)
    combined = join_slabs(own, suffix)
    lower = (prefix[1] - prefix[2][3] * combined[0]) / (1.0 - prefix[2][3] * combined[2][0])
    upper = (suffix[0] - suffix[2][0] * (own[1] - own[2][2] * lower)) / (
        1.0 - suffix[2][0] * own[2][3]
    )
    return lower, upper


def kernel(
    n, naz, R, NTL, NZL,
    v, rc, ac, kc, out,
    F, Y, Q, RCF, ACF, HA, PS, PR, RB0, RBE, RBI, TB, MA, MB, PHI, PSI, DP, DM, A0, SPK, CF, LU, ST,
    az_ss, az_rs, ax_ss, ax_rs, r0_ss, r0_rs, re_ss, re_rs, ri_ss, ri_rs, t_ss, t_rs,
):
    me = lax.axis_index("rad")
    az = lax.axis_index("az")
    ax = lax.axis_index("ax")
    left = lax.rem(az + naz - 1, naz)
    right = lax.rem(az + 1, naz)
    other = 1 - ax
    peers = [lax.rem(me + d, n) for d in range(1, n)]
    NI = NTL - 4

    barrier = pltpu.get_barrier_semaphore()
    for p in peers:
        pl.semaphore_signal(barrier, inc=1, device_id={"rad": p}, device_id_type=MESH)
    for p in (left, right):
        pl.semaphore_signal(barrier, inc=1, device_id={"az": p}, device_id_type=MESH)
    pl.semaphore_signal(barrier, inc=1, device_id={"ax": other}, device_id_type=MESH)
    pl.semaphore_wait(barrier, n + 2)

    def az_copy(s, side):
        if side == 0:
            src, dst, to = F.at[pl.ds(2, 2), pl.ds(PAD, R)], HA.at[s, 1], left
        else:
            src, dst, to = F.at[pl.ds(NTL, 2), pl.ds(PAD, R)], HA.at[s, 0], right
        return pltpu.make_async_remote_copy(
            src_ref=src, dst_ref=dst, send_sem=az_ss.at[s, side],
            recv_sem=az_rs.at[s, 1 - side], device_id={"az": to}, device_id_type=MESH)

    def ax_copy(s):
        return pltpu.make_async_remote_copy(
            src_ref=PS.at[s], dst_ref=PR.at[s], send_sem=ax_ss.at[s],
            recv_sem=ax_rs.at[s], device_id={"ax": other}, device_id_type=MESH)

    def rad_send(buf, ss, rs, d):
        return pltpu.make_async_remote_copy(
            src_ref=buf.at[me], dst_ref=buf.at[me], send_sem=ss.at[d],
            recv_sem=rs.at[me], device_id={"rad": peers[d]}, device_id_type=MESH)

    def rad_recv(buf, ss, rs, d):
        return pltpu.make_async_remote_copy(
            src_ref=buf.at[me], dst_ref=buf.at[peers[d]], send_sem=ss.at[d],
            recv_sem=rs.at[peers[d]], device_id={"rad": peers[d]}, device_id_type=MESH)

    lane = lax.broadcasted_iota(jnp.int32, (CH, 128), 1)

    def pack(s):
        for c in range(R // CH):
            rows = pl.ds(PAD + c * CH, CH)
            acc = jnp.zeros((CH, 128), F32)
            for j in range(NTL):
                edge = jnp.where(ax == 0, F[j + 2, rows, pl.ds(NZL - 128, 128)],
                                 F[j + 2, rows, pl.ds(0, 128)])
                acc = jnp.where(lane // 2 == j, pltpu.roll(edge, 2 * j + 2 * (1 - ax), 1), acc)
            PS[s, pl.ds(c * CH, CH), :] = acc

    TILES = NZL // 128

    def stage(ref, scale):
        def body(c, carry):
            rows = pl.ds(pl.multiple_of(c * 128, 128), 128)
            for i in range(TILES):
                x = ref[rows, pl.ds(128 * i, 128)].astype(F32)
                ST[i, rows, :] = x if scale is None else x * scale
            return carry

        lax.fori_loop(0, R * NTL // 128, body, 0)

    def split_read(i, j):
        return ST[i, pl.ds(j, R, stride=NTL), :]

    stage(v, None)
    for j in range(NTL):
        for i in range(TILES):
            F[j + 2, pl.ds(PAD, R), pl.ds(128 * i, 128)] = split_read(i, j)
    RB0[me, 0:NTL, :] = v[0:NTL, :]
    RB0[me, NTL : 2 * NTL, :] = v[(R - 1) * NTL : R * NTL, :]
    az_copy(0, 0).start()
    az_copy(0, 1).start()
    for d in range(n - 1):
        rad_send(RB0, r0_ss, r0_rs, d).start()
    pack(0)
    ax_copy(0).start()

    lane1 = lax.broadcasted_iota(jnp.int32, (1, 128), 1)
    ones = jnp.ones((1, 128), F32)

    def march(i, carry):
        phi, p, psi, m = carry
        k = R - 1 - i
        PHI[pl.ds(i, 1), :] = phi
        PSI[pl.ds(k, 1), :] = psi
        DM[pl.ds(k, 1), :] = m
        p = kc[2, pl.ds(i, 1), :] * phi + kc[5, pl.ds(i, 1), :] * p
        m = kc[6, pl.ds(k, 1), :] * psi + kc[7, pl.ds(k, 1), :] * m
        DP[pl.ds(i, 1), :] = p
        return phi + p, p, psi + m, m

    lax.fori_loop(0, R, march, (ones, ones, ones, ones))
    weight = 1.0 / (kc[1] * (DP[...] * PSI[...] + PHI[...] * DM[...]))
    at_i = lax.broadcasted_iota(jnp.int32, (R, R), 0)
    at_j = lax.broadcasted_iota(jnp.int32, (R, R), 1)
    upper_part = jnp.transpose(PSI[...] * weight)[0:R, :]
    lower_part = jnp.transpose(PHI[...] * weight)[0:R, :]
    inverse = jnp.where(at_i <= at_j, PHI[:, 0:R] * upper_part, PSI[:, 0:R] * lower_part)
    high = inverse.astype(jnp.bfloat16)
    MA[:, 0:R] = high
    MA[:, R : 2 * R] = high
    MB[...] = (inverse - high.astype(F32)).astype(jnp.bfloat16)
    SPK[0] = -kc[0, 0:1, :] * jnp.broadcast_to(inverse[:, 0:1], (R, 128))
    SPK[1] = -kc[1, R - 1 : R, :] * jnp.broadcast_to(inverse[:, R - 1 : R], (R, 128))
    A0[...] = 2.0 - 30.0 * (0.25 / 12.0) - 30.0 * kc[4]
    TB[me, 0:1, :] = SPK[0, 0:1, :]
    TB[me, 1:2, :] = SPK[1, 0:1, :]
    TB[me, 2:3, :] = SPK[0, R - 1 : R, :]
    TB[me, 3:4, :] = SPK[1, R - 1 : R, :]
    TB[me, 4:8, :] = jnp.zeros((4, 128), F32)
    for d in range(n - 1):
        rad_send(TB, t_ss, t_rs, d).start()

    for src, dst, scale in ((rc, RCF, -0.5), (ac, ACF, -1.0 / 12.0)):
        stage(src, scale)
        for j in range(NTL):
            for i in range(TILES):
                dst[j, :, pl.ds(128 * i, 128)] = split_read(i, j)

    for d in range(n - 1):
        rad_recv(RB0, r0_ss, r0_rs, d).wait_recv()
    below = jnp.maximum(me - 1, 0)
    above = jnp.minimum(me + 1, n - 1)
    low0 = jnp.where(me > 0, RB0[below, NTL : 2 * NTL, :], 0.0)
    high0 = jnp.where(me < n - 1, RB0[above, 0:NTL, :], 0.0)
    for j in range(NTL):
        F[j + 2, PAD - 1 : PAD, :] = low0[j : j + 1, :]
        F[j + 2, PAD + R : PAD + R + 1, :] = high0[j : j + 1, :]

    for d in range(n - 1):
        rad_recv(TB, t_ss, t_rs, d).wait_recv()
    members = []
    for k in range(n):
        members.append((
            jnp.where(lane1 == 2 * k, 1.0, 0.0),
            jnp.where(lane1 == 2 * k + 1, 1.0, 0.0),
            tuple(TB[k, q : q + 1, :] for q in range(4)),
        ))
    lower_map, upper_map = interface_rows(members, me, n)
    for m in range(2 * n):
        for h, vec in enumerate((lower_map, upper_map)):
            val = jnp.sum(jnp.where(lane1 == m, vec, 0.0), axis=1, keepdims=True)
            CF[h, m // 2, m % 2 : m % 2 + 1, :] = jnp.broadcast_to(val, (1, 128))

    ml = jnp.where(ax == 1, 1.0, 0.0).astype(F32)
    mr = jnp.where(ax == 0, 1.0, 0.0).astype(F32)

    def wide(x):
        return jnp.concatenate([x] * (NZL // 128), axis=1)

    def solve_one(s, j):
        for c in range(R // CH):
            r0 = c * CH
            rows = pl.ds(PAD + r0, CH)
            f = F[j + 2, rows, :]
            m1, m2 = F[j + 1, rows, :], F[j, rows, :]
            p1, p2 = F[j + 3, rows, :], F[j + 4, rows, :]
            lo = F[j + 2, pl.ds(PAD + r0 - 1, CH), :]
            up = F[j + 2, pl.ds(PAD + r0 + 1, CH), :]
            ct = wide(kc[3, pl.ds(r0, CH), :])
            cl = wide(kc[4, pl.ds(r0, CH), :])
            halo = pltpu.roll(PR[s, pl.ds(r0, CH), :], 128 - 2 * j, 1)
            halo1 = pltpu.roll(halo, 127, 1)
            halo2 = pltpu.roll(halo, 126, 1)
            tiles = [f[:, i * 128 : (i + 1) * 128] for i in range(NZL // 128)]
            shifted = {}
            for k in (1, 2):
                down = [pltpu.roll(t, k, 1) for t in tiles]
                edge = ml * (halo1 if k == 1 else halo)
                shifted[-k] = jnp.concatenate([
                    jnp.where(lane < k, edge if i == 0 else down[i - 1], down[i])
                    for i in range(len(tiles))], axis=1)
                rise = [pltpu.roll(t, 128 - k, 1) for t in tiles]
                edge = mr * (halo1 if k == 1 else halo2)
                shifted[k] = jnp.concatenate([
                    jnp.where(lane >= 128 - k,
                              edge if i == len(tiles) - 1 else rise[i + 1], rise[i])
                    for i in range(len(tiles))], axis=1)
            z1d = shifted[1] - shifted[-1]
            z2d = shifted[2] - shifted[-2]
            z1s = shifted[1] + shifted[-1]
            z2s = shifted[2] + shifted[-2]
            a0 = wide(A0[pl.ds(r0, CH), :])
            q = (
                f * (a0 + ct * (8.0 * (p1 - m1) - (p2 - m2)))
                + cl * (16.0 * (p1 + m1) - (p2 + m2))
                + RCF[j, pl.ds(r0, CH), :] * (up - lo)
                + ACF[j, pl.ds(r0, CH), :] * (8.0 * z1d - z2d)
                + (0.25 / 12.0) * (16.0 * z1s - z2s)
            )
            qh = q.astype(jnp.bfloat16)
            cols = pl.ds(pl.multiple_of(j * NZL, NZL), NZL)
            Q[pl.ds(r0, CH), cols] = qh
            Q[pl.ds(R + r0, CH), cols] = (q - qh.astype(F32)).astype(jnp.bfloat16)

    def multiply(start, width):
        cols = pl.ds(start, width)
        y = jnp.dot(MA[...], Q[:, cols], preferred_element_type=F32)
        Y[:, cols] = y + jnp.dot(MB[...], Q[0:R, cols], preferred_element_type=F32)

    def edge_of(e):
        return e + (NTL - 4) * (e // 2)

    def finish(s, j):
        cols = pl.ds(pl.multiple_of(j * NZL, NZL), NZL)
        low = LU[0:1, cols]
        high = LU[1:2, cols]
        for c in range(R // CH):
            rows = pl.ds(PAD + c * CH, CH)
            F[j + 2, rows, :] = (
                Y[pl.ds(c * CH, CH), cols]
                - wide(SPK[0, pl.ds(c * CH, CH), :]) * low
                - wide(SPK[1, pl.ds(c * CH, CH), :]) * high
                - F[j + 2, rows, :]
            )
        F[j + 2, PAD - 1 : PAD, :] = low - F[j + 2, PAD - 1 : PAD, :]
        F[j + 2, PAD + R : PAD + R + 1, :] = high - F[j + 2, PAD + R : PAD + R + 1, :]

    def ends(buf, s, width):
        res = []
        for h in range(2):
            total = None
            for k in range(n):
                coef = jnp.concatenate([CF[h, k]] * (width // 128), axis=1)
                term = coef * buf[s, k]
                total = term if total is None else total + term
            res.append(total[0:1, :] + total[1:2, :])
        return res

    def step(s, carry):
        ax_copy(s).wait_recv()

        def inner(jj, c):
            solve_one(s, jj + 2)
            return c

        lax.fori_loop(0, NI, inner, 0)
        multiply(2 * NZL, NI * NZL)
        mid = pl.ds(2 * NZL, NI * NZL)
        RBI[s, me, 0:1, :] = Y[0:1, mid]
        RBI[s, me, 1:2, :] = Y[R - 1 : R, mid]
        for d in range(n - 1):
            rad_send(RBI.at[s], ri_ss.at[s], ri_rs.at[s], d).start()
        for side in range(2):
            az_copy(s, side).wait_recv()
        for i in range(2):
            F[i, pl.ds(PAD, R), :] = HA[s, 0, i]
            F[NTL + 2 + i, pl.ds(PAD, R), :] = HA[s, 1, i]

        def outer(e, c):
            solve_one(s, edge_of(e))
            return c

        lax.fori_loop(0, 4, outer, 0)
        two = 2 * NZL
        for i, start in enumerate((0, (NTL - 2) * NZL)):
            multiply(start, two)
            RBE[s, me, 0:1, i * two : (i + 1) * two] = Y[0:1, start : start + two]
            RBE[s, me, 1:2, i * two : (i + 1) * two] = Y[R - 1 : R, start : start + two]
        for d in range(n - 1):
            rad_send(RBE.at[s], re_ss.at[s], re_rs.at[s], d).start()
        for side in range(2):
            az_copy(s, side).wait_send()
        for d in range(n - 1):
            rad_recv(RBE.at[s], re_ss.at[s], re_rs.at[s], d).wait_recv()
        for h, row in enumerate(ends(RBE, s, 4 * NZL)):
            LU[h : h + 1, 0:two] = row[:, 0:two]
            LU[h : h + 1, (NTL - 2) * NZL : NTL * NZL] = row[:, two : 2 * two]

        def outer2(e, c):
            finish(s, edge_of(e))
            return c

        lax.fori_loop(0, 4, outer2, 0)

        @pl.when(s < STEPS - 1)
        def _():
            az_copy(s + 1, 0).start()
            az_copy(s + 1, 1).start()

        for d in range(n - 1):
            rad_recv(RBI.at[s], ri_ss.at[s], ri_rs.at[s], d).wait_recv()
        for h, row in enumerate(ends(RBI, s, NI * NZL)):
            LU[h : h + 1, mid] = row

        def inner2(jj, c):
            finish(s, jj + 2)
            return c

        lax.fori_loop(0, NI, inner2, 0)

        @pl.when(s < STEPS - 1)
        def _():
            pack(s + 1)
            ax_copy(s + 1).start()

        ax_copy(s).wait_send()
        for d in range(n - 1):
            rad_send(RBE.at[s], re_ss.at[s], re_rs.at[s], d).wait_send()
            rad_send(RBI.at[s], ri_ss.at[s], ri_rs.at[s], d).wait_send()
        return carry

    lax.fori_loop(0, STEPS, step, 0)
    for j in range(NTL):
        for i in range(NZL // 128):
            ST[i, pl.ds(j, R, stride=NTL), :] = F[j + 2, pl.ds(PAD, R), pl.ds(128 * i, 128)]

    def unstage(c, carry):
        rows = pl.ds(pl.multiple_of(c * 128, 128), 128)
        for i in range(TILES):
            out[rows, pl.ds(128 * i, 128)] = ST[i, rows, :]
        return carry

    lax.fori_loop(0, R * NTL // 128, unstage, 0)
    for d in range(n - 1):
        rad_send(RB0, r0_ss, r0_rs, d).wait_send()
        rad_send(TB, t_ss, t_rs, d).wait_send()


def local(n, naz, velocity, radial_courant, axial_courant, radial_diffusion):
    R, NTL, NZL = velocity.shape
    position = (lax.axis_index("rad") * R).astype(F32) + jnp.arange(R).astype(F32)
    spacing = 1.0 / (NR + 1)
    radius = 1.0 + (position + 1.0) * spacing
    inward = radial_diffusion * (radius - 0.5 * spacing) / radius
    outward = radial_diffusion * (radius + 0.5 * spacing) / radius
    sink = radial_diffusion * spacing * spacing / (radius * radius)
    grow = 1.0 + sink
    kc = jnp.stack([inward, outward, grow / outward, -(0.25 / 12.0) / radius,
                    (0.25 / 12.0) / (radius * radius), inward / outward,
                    grow / inward, outward / inward])
    kc = jnp.broadcast_to(kc[:, :, None], (8, R, 128))
    flat = lambda a: a.reshape(R * NTL, NZL)
    S = STEPS
    dma = pltpu.SemaphoreType.DMA
    res = pl.pallas_call(
        functools.partial(kernel, n, naz, R, NTL, NZL),
        out_shape=jax.ShapeDtypeStruct((R * NTL, NZL), F32),
        in_specs=[pl.BlockSpec(memory_space=pltpu.VMEM)] * 4,
        out_specs=pl.BlockSpec(memory_space=pltpu.VMEM),
        scratch_shapes=[
            pltpu.VMEM((NTL + 4, R + 2 * PAD, NZL), F32),
            pltpu.VMEM((R, NTL * NZL), F32),
            pltpu.VMEM((2 * R, NTL * NZL), jnp.bfloat16),
            pltpu.VMEM((NTL, R, NZL), F32),
            pltpu.VMEM((NTL, R, NZL), F32),
            pltpu.VMEM((S, 2, 2, R, NZL), F32),
            pltpu.VMEM((S, R, 128), F32),
            pltpu.VMEM((S, R, 128), F32),
            pltpu.VMEM((n, 2 * NTL, NZL), F32),
            pltpu.VMEM((S, n, 2, 4 * NZL), F32),
            pltpu.VMEM((S, n, 2, (NTL - 4) * NZL), F32),
            pltpu.VMEM((n, 8, 128), F32),
            pltpu.VMEM((R, 2 * R), jnp.bfloat16),
            pltpu.VMEM((R, R), jnp.bfloat16),
            pltpu.VMEM((R, 128), F32),
            pltpu.VMEM((R, 128), F32),
            pltpu.VMEM((R, 128), F32),
            pltpu.VMEM((R, 128), F32),
            pltpu.VMEM((R, 128), F32),
            pltpu.VMEM((2, R, 128), F32),
            pltpu.VMEM((2, n, 2, 128), F32),
            pltpu.VMEM((2, NTL * NZL), F32),
            pltpu.VMEM((NZL // 128, R * NTL, 128), F32),
            dma((S, 2)), dma((S, 2)), dma((S,)), dma((S,)),
            dma((n,)), dma((n,)), dma((S, n)), dma((S, n)),
            dma((S, n)), dma((S, n)), dma((n,)), dma((n,)),
        ],
        compiler_params=pltpu.CompilerParams(
            collective_id=0, has_side_effects=True, vmem_limit_bytes=48 * 1024 * 1024),
    )(flat(velocity), flat(radial_courant), flat(axial_courant), kc)
    return res.reshape(R, NTL, NZL)


def solution(mesh):
    return jax.shard_map(
        functools.partial(local, mesh.shape["rad"], mesh.shape["az"]),
        mesh=mesh,
        in_specs=(P("rad", "az", "ax"), P("rad", "az", "ax"), P("rad", "az", "ax"), P("rad")),
        out_specs=P("rad", "az", "ax"),
        check_vma=False,
    )
```

```python
import functools

import jax
import jax.numpy as jnp
from jax import lax
from jax.experimental import pallas as pl
from jax.experimental.pallas import tpu as pltpu
from jax.sharding import PartitionSpec as P

NR = 512
STEPS = 6
F32 = jnp.float32
MESH = pl.DeviceIdType.MESH
PAD = 8
CH = 32


def join_slabs(left, right):
    head_l, tail_l, tl = left
    head_r, tail_r, tr = right
    divisor = 1.0 - tl[3] * tr[0]
    mid_value = (tail_l - tl[3] * head_r) / divisor
    mid_left = tl[2] / divisor
    mid_right = -tl[3] * tr[1] / divisor
    next_value = head_r - tr[0] * mid_value
    next_left = -tr[0] * mid_left
    next_right = tr[1] - tr[0] * mid_right
    return (
        head_l - tl[1] * next_value,
        tail_r - tr[2] * mid_value,
        (
            tl[0] - tl[1] * next_left,
            -tl[1] * next_right,
            -tr[2] * mid_left,
            tr[3] - tr[2] * mid_right,
        ),
    )


def interface_rows(members, me, n):
    zero = jnp.zeros_like(members[0][0])
    identity = (zero, zero, (zero, zero - 1.0, zero - 1.0, zero))

    def choose(cond, a, b):
        return jax.tree.map(lambda x, y: jnp.where(cond, x, y), a, b)

    prefix = identity
    own = members[0]
    for k in range(n):
        own = choose(k == me, members[k], own)
        prefix = choose(k < me, join_slabs(prefix, members[k]), prefix)
    suffix = identity
    for k in range(n - 1, -1, -1):
        suffix = choose(k > me, join_slabs(members[k], suffix), suffix)
    combined = join_slabs(own, suffix)
    lower = (prefix[1] - prefix[2][3] * combined[0]) / (1.0 - prefix[2][3] * combined[2][0])
    upper = (suffix[0] - suffix[2][0] * (own[1] - own[2][2] * lower)) / (
        1.0 - suffix[2][0] * own[2][3]
    )
    return lower, upper


def kernel(
    n, naz, R, NTL, NZL,
    v, rc, ac, kc, out,
    F, Y, YE, Q, RCF, ACF, HA, PS, PR, RB0, RBE, RBI, TB, MA, MB, PHI, PSI, DP, DM, A0, SPK, CF, LU, ST,
    az_ss, az_rs, ax_ss, ax_rs, r0_ss, r0_rs, re_ss, re_rs, ri_ss, ri_rs, t_ss, t_rs,
):
    me = lax.axis_index("rad")
    az = lax.axis_index("az")
    ax = lax.axis_index("ax")
    left = lax.rem(az + naz - 1, naz)
    right = lax.rem(az + 1, naz)
    other = 1 - ax
    peers = [lax.rem(me + d, n) for d in range(1, n)]
    NI = NTL - 4

    barrier = pltpu.get_barrier_semaphore()
    for p in peers:
        pl.semaphore_signal(barrier, inc=1, device_id={"rad": p}, device_id_type=MESH)
    for p in (left, right):
        pl.semaphore_signal(barrier, inc=1, device_id={"az": p}, device_id_type=MESH)
    pl.semaphore_signal(barrier, inc=1, device_id={"ax": other}, device_id_type=MESH)
    pl.semaphore_wait(barrier, n + 2)

    def az_copy(s, half, side):
        first, to = ((2, left), (NTL, right))[side]
        return pltpu.make_async_remote_copy(
            src_ref=F.at[pl.ds(first, 2), pl.ds(PAD, R), pl.ds(128 * half, 128)],
            dst_ref=HA.at[s, half, 1 - side], send_sem=az_ss.at[s, half, side],
            recv_sem=az_rs.at[s, half, 1 - side], device_id={"az": to}, device_id_type=MESH)

    def ax_copy(s):
        return pltpu.make_async_remote_copy(
            src_ref=PS.at[s], dst_ref=PR.at[s], send_sem=ax_ss.at[s],
            recv_sem=ax_rs.at[s], device_id={"ax": other}, device_id_type=MESH)

    def rad_send(buf, ss, rs, d):
        return pltpu.make_async_remote_copy(
            src_ref=buf.at[me], dst_ref=buf.at[me], send_sem=ss.at[d],
            recv_sem=rs.at[me], device_id={"rad": peers[d]}, device_id_type=MESH)

    def rad_recv(buf, ss, rs, d):
        return pltpu.make_async_remote_copy(
            src_ref=buf.at[me], dst_ref=buf.at[peers[d]], send_sem=ss.at[d],
            recv_sem=rs.at[peers[d]], device_id={"rad": peers[d]}, device_id_type=MESH)

    lane = lax.broadcasted_iota(jnp.int32, (CH, 128), 1)

    def pack(s):
        for c in range(R // CH):
            rows = pl.ds(PAD + c * CH, CH)
            acc = jnp.zeros((CH, 128), F32)
            for j in range(NTL):
                edge = jnp.where(ax == 0, F[j + 2, rows, pl.ds(NZL - 128, 128)],
                                 F[j + 2, rows, pl.ds(0, 128)])
                acc = jnp.where(lane // 2 == j, pltpu.roll(edge, 2 * j + 2 * (1 - ax), 1), acc)
            PS[s, pl.ds(c * CH, CH), :] = acc

    TILES = NZL // 128

    def stage(ref, scale):
        def body(c, carry):
            rows = pl.ds(pl.multiple_of(c * 128, 128), 128)
            for i in range(TILES):
                x = ref[rows, pl.ds(128 * i, 128)].astype(F32)
                ST[i, rows, :] = x if scale is None else x * scale
            return carry

        lax.fori_loop(0, R * NTL // 128, body, 0)

    def split_read(i, j):
        return ST[i, pl.ds(j, R, stride=NTL), :]

    stage(v, None)
    for j in range(NTL):
        for i in range(TILES):
            F[j + 2, pl.ds(PAD, R), pl.ds(128 * i, 128)] = split_read(i, j)
    RB0[me, 0:NTL, :] = v[0:NTL, :]
    RB0[me, NTL : 2 * NTL, :] = v[(R - 1) * NTL : R * NTL, :]
    for half in range(NZL // 128):
        az_copy(0, half, 0).start()
        az_copy(0, half, 1).start()
    for d in range(n - 1):
        rad_send(RB0, r0_ss, r0_rs, d).start()
    pack(0)
    ax_copy(0).start()

    lane1 = lax.broadcasted_iota(jnp.int32, (1, 128), 1)
    ones = jnp.ones((1, 128), F32)

    def march(i, carry):
        phi, p, psi, m = carry
        k = R - 1 - i
        PHI[pl.ds(i, 1), :] = phi
        PSI[pl.ds(k, 1), :] = psi
        DM[pl.ds(k, 1), :] = m
        p = kc[2, pl.ds(i, 1), :] * phi + kc[5, pl.ds(i, 1), :] * p
        m = kc[6, pl.ds(k, 1), :] * psi + kc[7, pl.ds(k, 1), :] * m
        DP[pl.ds(i, 1), :] = p
        return phi + p, p, psi + m, m

    lax.fori_loop(0, R, march, (ones, ones, ones, ones))
    weight = 1.0 / (kc[1] * (DP[...] * PSI[...] + PHI[...] * DM[...]))
    at_i = lax.broadcasted_iota(jnp.int32, (R, R), 0)
    at_j = lax.broadcasted_iota(jnp.int32, (R, R), 1)
    upper_part = jnp.transpose(PSI[...] * weight)[0:R, :]
    lower_part = jnp.transpose(PHI[...] * weight)[0:R, :]
    inverse = jnp.where(at_i <= at_j, PHI[:, 0:R] * upper_part, PSI[:, 0:R] * lower_part)
    high = inverse.astype(jnp.bfloat16)
    MA[:, 0:R] = high
    MA[:, R : 2 * R] = high
    MB[...] = (inverse - high.astype(F32)).astype(jnp.bfloat16)
    SPK[0] = -kc[0, 0:1, :] * jnp.broadcast_to(inverse[:, 0:1], (R, 128))
    SPK[1] = -kc[1, R - 1 : R, :] * jnp.broadcast_to(inverse[:, R - 1 : R], (R, 128))
    A0[...] = 2.0 - 30.0 * (0.25 / 12.0) - 30.0 * kc[4]
    TB[me, 0:1, :] = SPK[0, 0:1, :]
    TB[me, 1:2, :] = SPK[1, 0:1, :]
    TB[me, 2:3, :] = SPK[0, R - 1 : R, :]
    TB[me, 3:4, :] = SPK[1, R - 1 : R, :]
    TB[me, 4:8, :] = jnp.zeros((4, 128), F32)
    for d in range(n - 1):
        rad_send(TB, t_ss, t_rs, d).start()

    for src, dst, scale in ((rc, RCF, -0.5), (ac, ACF, -1.0 / 12.0)):
        stage(src, scale)
        for j in range(NTL):
            for i in range(TILES):
                dst[j, :, pl.ds(128 * i, 128)] = split_read(i, j)

    for d in range(n - 1):
        rad_recv(RB0, r0_ss, r0_rs, d).wait_recv()
    below = jnp.maximum(me - 1, 0)
    above = jnp.minimum(me + 1, n - 1)
    low0 = jnp.where(me > 0, RB0[below, NTL : 2 * NTL, :], 0.0)
    high0 = jnp.where(me < n - 1, RB0[above, 0:NTL, :], 0.0)
    for j in range(NTL):
        F[j + 2, PAD - 1 : PAD, :] = low0[j : j + 1, :]
        F[j + 2, PAD + R : PAD + R + 1, :] = high0[j : j + 1, :]

    for d in range(n - 1):
        rad_recv(TB, t_ss, t_rs, d).wait_recv()
    members = []
    for k in range(n):
        members.append((
            jnp.where(lane1 == 2 * k, 1.0, 0.0),
            jnp.where(lane1 == 2 * k + 1, 1.0, 0.0),
            tuple(TB[k, q : q + 1, :] for q in range(4)),
        ))
    lower_map, upper_map = interface_rows(members, me, n)
    for m in range(2 * n):
        for h, vec in enumerate((lower_map, upper_map)):
            val = jnp.sum(jnp.where(lane1 == m, vec, 0.0), axis=1, keepdims=True)
            CF[h, m // 2, m % 2 : m % 2 + 1, :] = jnp.broadcast_to(val, (1, 128))

    ml = jnp.where(ax == 1, 1.0, 0.0).astype(F32)
    mr = jnp.where(ax == 0, 1.0, 0.0).astype(F32)

    def wide(x):
        return jnp.concatenate([x] * (NZL // 128), axis=1)

    def solve_one(s, j, inner):
        for c in range(R // CH):
            r0 = c * CH
            rows = pl.ds(PAD + r0, CH)
            f = F[j + 2, rows, :]
            lo = F[j + 2, pl.ds(PAD + r0 - 1, CH), :]
            up = F[j + 2, pl.ds(PAD + r0 + 1, CH), :]
            ct = wide(kc[3, pl.ds(r0, CH), :])
            cl = wide(kc[4, pl.ds(r0, CH), :])
            halo = pltpu.roll(PR[s, pl.ds(r0, CH), :], 128 - 2 * j, 1)
            halo1 = pltpu.roll(halo, 127, 1)
            halo2 = pltpu.roll(halo, 126, 1)
            tiles = [f[:, i * 128 : (i + 1) * 128] for i in range(NZL // 128)]
            shifted = {}
            for k in (1, 2):
                down = [pltpu.roll(t, k, 1) for t in tiles]
                edge = ml * (halo1 if k == 1 else halo)
                shifted[-k] = jnp.concatenate([
                    jnp.where(lane < k, edge if i == 0 else down[i - 1], down[i])
                    for i in range(len(tiles))], axis=1)
                rise = [pltpu.roll(t, 128 - k, 1) for t in tiles]
                edge = mr * (halo1 if k == 1 else halo2)
                shifted[k] = jnp.concatenate([
                    jnp.where(lane >= 128 - k,
                              edge if i == len(tiles) - 1 else rise[i + 1], rise[i])
                    for i in range(len(tiles))], axis=1)
            z1d = shifted[1] - shifted[-1]
            z2d = shifted[2] - shifted[-2]
            z1s = shifted[1] + shifted[-1]
            z2s = shifted[2] + shifted[-2]
            a0 = wide(A0[pl.ds(r0, CH), :])
            q = (
                f * a0
                + RCF[j, pl.ds(r0, CH), :] * (up - lo)
                + ACF[j, pl.ds(r0, CH), :] * (8.0 * z1d - z2d)
                + (0.25 / 12.0) * (16.0 * z1s - z2s)
            )
            cols = pl.ds(pl.multiple_of(j * NZL, NZL), NZL)
            if not inner:
                Y[pl.ds(r0, CH), cols] = q
                continue
            m1, m2 = F[j + 1, rows, :], F[j, rows, :]
            p1, p2 = F[j + 3, rows, :], F[j + 4, rows, :]
            q = q + f * (ct * (8.0 * (p1 - m1) - (p2 - m2)))
            q = q + cl * (16.0 * (p1 + m1) - (p2 + m2))
            qh = q.astype(jnp.bfloat16)
            Q[pl.ds(r0, CH), cols] = qh
            Q[pl.ds(R + r0, CH), cols] = (q - qh.astype(F32)).astype(jnp.bfloat16)

    def edge_terms(half, e):
        j = edge_of(e)
        lanes = pl.ds(128 * half, 128)
        cols = pl.ds(pl.multiple_of(j * NZL + 128 * half, 128), 128)
        packed = pl.ds(pl.multiple_of(e * 128, 128), 128)
        for c in range(R // CH):
            r0 = c * CH
            rows = pl.ds(PAD + r0, CH)
            f = F[j + 2, rows, lanes]
            m1, m2 = F[j + 1, rows, lanes], F[j, rows, lanes]
            p1, p2 = F[j + 3, rows, lanes], F[j + 4, rows, lanes]
            q = (
                Y[pl.ds(r0, CH), cols]
                + f * (kc[3, pl.ds(r0, CH), :] * (8.0 * (p1 - m1) - (p2 - m2)))
                + kc[4, pl.ds(r0, CH), :] * (16.0 * (p1 + m1) - (p2 + m2))
            )
            qh = q.astype(jnp.bfloat16)
            Q[pl.ds(r0, CH), packed] = qh
            Q[pl.ds(R + r0, CH), packed] = (q - qh.astype(F32)).astype(jnp.bfloat16)

    def edge_finish(half, e, low, high):
        j = edge_of(e)
        lanes = pl.ds(128 * half, 128)
        for c in range(R // CH):
            rows = pl.ds(PAD + c * CH, CH)
            here = pl.ds(c * CH, CH)
            F[j + 2, rows, lanes] = (
                YE[here, pl.ds(e * 128, 128)] - SPK[0, here, :] * low
                - SPK[1, here, :] * high - F[j + 2, rows, lanes]
            )
        F[j + 2, PAD - 1 : PAD, lanes] = low - F[j + 2, PAD - 1 : PAD, lanes]
        F[j + 2, PAD + R : PAD + R + 1, lanes] = high - F[j + 2, PAD + R : PAD + R + 1, lanes]

    def multiply(start, width):
        cols = pl.ds(start, width)
        y = jnp.dot(MA[...], Q[:, cols], preferred_element_type=F32)
        Y[:, cols] = y + jnp.dot(MB[...], Q[0:R, cols], preferred_element_type=F32)

    def edge_of(e):
        return e + (NTL - 4) * (e // 2)

    def finish(s, j):
        cols = pl.ds(pl.multiple_of(j * NZL, NZL), NZL)
        low = LU[0:1, cols]
        high = LU[1:2, cols]
        for c in range(R // CH):
            rows = pl.ds(PAD + c * CH, CH)
            F[j + 2, rows, :] = (
                Y[pl.ds(c * CH, CH), cols]
                - wide(SPK[0, pl.ds(c * CH, CH), :]) * low
                - wide(SPK[1, pl.ds(c * CH, CH), :]) * high
                - F[j + 2, rows, :]
            )
        F[j + 2, PAD - 1 : PAD, :] = low - F[j + 2, PAD - 1 : PAD, :]
        F[j + 2, PAD + R : PAD + R + 1, :] = high - F[j + 2, PAD + R : PAD + R + 1, :]

    def ends(buf, s, width):
        res = []
        for h in range(2):
            total = None
            for k in range(n):
                coef = jnp.concatenate([CF[h, k]] * (width // 128), axis=1)
                term = coef * buf[(*s, k)]
                total = term if total is None else total + term
            res.append(total[0:1, :] + total[1:2, :])
        return res

    def step(s, carry):
        ax_copy(s).wait_recv()

        def inner(jj, c):
            solve_one(s, jj + 2, True)
            return c

        lax.fori_loop(0, NI, inner, 0)
        multiply(2 * NZL, NI * NZL)
        mid = pl.ds(2 * NZL, NI * NZL)
        RBI[s, me, 0:1, :] = Y[0:1, mid]
        RBI[s, me, 1:2, :] = Y[R - 1 : R, mid]
        for d in range(n - 1):
            rad_send(RBI.at[s], ri_ss.at[s], ri_rs.at[s], d).start()
        def outer(e, c):
            solve_one(s, edge_of(e), False)
            return c

        lax.fori_loop(0, 4, outer, 0)
        for half in range(NZL // 128):
            lanes = pl.ds(128 * half, 128)
            for side in range(2):
                az_copy(s, half, side).wait_recv()
            for i in range(2):
                F[i, pl.ds(PAD, R), lanes] = HA[s, half, 0, i]
                F[NTL + 2 + i, pl.ds(PAD, R), lanes] = HA[s, half, 1, i]
            for e in range(4):
                edge_terms(half, e)
            y = jnp.dot(MA[...], Q[:, 0:512], preferred_element_type=F32)
            y = y + jnp.dot(MB[...], Q[0:R, 0:512], preferred_element_type=F32)
            YE[...] = y
            RBE[s, half, me, 0:1, :] = y[0:1, :]
            RBE[s, half, me, 1:2, :] = y[R - 1 : R, :]
            buf, ss, rs = RBE.at[s, half], re_ss.at[s, half], re_rs.at[s, half]
            for d in range(n - 1):
                rad_send(buf, ss, rs, d).start()
            for side in range(2):
                az_copy(s, half, side).wait_send()
            for d in range(n - 1):
                rad_recv(buf, ss, rs, d).wait_recv()
            low, high = ends(RBE, (s, half), 512)
            for e in range(4):
                edge_finish(half, e, low[:, e * 128 : (e + 1) * 128],
                            high[:, e * 128 : (e + 1) * 128])

            @pl.when(s < STEPS - 1)
            def _():
                az_copy(s + 1, half, 0).start()
                az_copy(s + 1, half, 1).start()

        for d in range(n - 1):
            rad_recv(RBI.at[s], ri_ss.at[s], ri_rs.at[s], d).wait_recv()
        for h, row in enumerate(ends(RBI, (s,), NI * NZL)):
            LU[h : h + 1, mid] = row

        def inner2(jj, c):
            finish(s, jj + 2)
            return c

        lax.fori_loop(0, NI, inner2, 0)

        @pl.when(s < STEPS - 1)
        def _():
            pack(s + 1)
            ax_copy(s + 1).start()

        ax_copy(s).wait_send()
        for d in range(n - 1):
            for half in range(NZL // 128):
                rad_send(RBE.at[s, half], re_ss.at[s, half], re_rs.at[s, half], d).wait_send()
            rad_send(RBI.at[s], ri_ss.at[s], ri_rs.at[s], d).wait_send()
        return carry

    lax.fori_loop(0, STEPS, step, 0)
    for j in range(NTL):
        for i in range(NZL // 128):
            ST[i, pl.ds(j, R, stride=NTL), :] = F[j + 2, pl.ds(PAD, R), pl.ds(128 * i, 128)]

    def unstage(c, carry):
        rows = pl.ds(pl.multiple_of(c * 128, 128), 128)
        for i in range(TILES):
            out[rows, pl.ds(128 * i, 128)] = ST[i, rows, :]
        return carry

    lax.fori_loop(0, R * NTL // 128, unstage, 0)
    for d in range(n - 1):
        rad_send(RB0, r0_ss, r0_rs, d).wait_send()
        rad_send(TB, t_ss, t_rs, d).wait_send()


def local(n, naz, velocity, radial_courant, axial_courant, radial_diffusion):
    R, NTL, NZL = velocity.shape
    position = (lax.axis_index("rad") * R).astype(F32) + jnp.arange(R).astype(F32)
    spacing = 1.0 / (NR + 1)
    radius = 1.0 + (position + 1.0) * spacing
    inward = radial_diffusion * (radius - 0.5 * spacing) / radius
    outward = radial_diffusion * (radius + 0.5 * spacing) / radius
    sink = radial_diffusion * spacing * spacing / (radius * radius)
    grow = 1.0 + sink
    kc = jnp.stack([inward, outward, grow / outward, -(0.25 / 12.0) / radius,
                    (0.25 / 12.0) / (radius * radius), inward / outward,
                    grow / inward, outward / inward])
    kc = jnp.broadcast_to(kc[:, :, None], (8, R, 128))
    flat = lambda a: a.reshape(R * NTL, NZL)
    S = STEPS
    dma = pltpu.SemaphoreType.DMA
    res = pl.pallas_call(
        functools.partial(kernel, n, naz, R, NTL, NZL),
        out_shape=jax.ShapeDtypeStruct((R * NTL, NZL), F32),
        in_specs=[pl.BlockSpec(memory_space=pltpu.VMEM)] * 4,
        out_specs=pl.BlockSpec(memory_space=pltpu.VMEM),
        scratch_shapes=[
            pltpu.VMEM((NTL + 4, R + 2 * PAD, NZL), F32),
            pltpu.VMEM((R, NTL * NZL), F32),
            pltpu.VMEM((R, 512), F32),
            pltpu.VMEM((2 * R, NTL * NZL), jnp.bfloat16),
            pltpu.VMEM((NTL, R, NZL), F32),
            pltpu.VMEM((NTL, R, NZL), F32),
            pltpu.VMEM((S, NZL // 128, 2, 2, R, 128), F32),
            pltpu.VMEM((S, R, 128), F32),
            pltpu.VMEM((S, R, 128), F32),
            pltpu.VMEM((n, 2 * NTL, NZL), F32),
            pltpu.VMEM((S, NZL // 128, n, 2, 512), F32),
            pltpu.VMEM((S, n, 2, (NTL - 4) * NZL), F32),
            pltpu.VMEM((n, 8, 128), F32),
            pltpu.VMEM((R, 2 * R), jnp.bfloat16),
            pltpu.VMEM((R, R), jnp.bfloat16),
            pltpu.VMEM((R, 128), F32),
            pltpu.VMEM((R, 128), F32),
            pltpu.VMEM((R, 128), F32),
            pltpu.VMEM((R, 128), F32),
            pltpu.VMEM((R, 128), F32),
            pltpu.VMEM((2, R, 128), F32),
            pltpu.VMEM((2, n, 2, 128), F32),
            pltpu.VMEM((2, NTL * NZL), F32),
            pltpu.VMEM((NZL // 128, R * NTL, 128), F32),
            dma((S, NZL // 128, 2)), dma((S, NZL // 128, 2)), dma((S,)), dma((S,)),
            dma((n,)), dma((n,)), dma((S, NZL // 128, n)), dma((S, NZL // 128, n)),
            dma((S, n)), dma((S, n)), dma((n,)), dma((n,)),
        ],
        compiler_params=pltpu.CompilerParams(
            collective_id=0, has_side_effects=True, vmem_limit_bytes=48 * 1024 * 1024),
    )(flat(velocity), flat(radial_courant), flat(axial_courant), kc)
    return res.reshape(R, NTL, NZL)


def solution(mesh):
    return jax.shard_map(
        functools.partial(local, mesh.shape["rad"], mesh.shape["az"]),
        mesh=mesh,
        in_specs=(P("rad", "az", "ax"), P("rad", "az", "ax"), P("rad", "az", "ax"), P("rad")),
        out_specs=P("rad", "az", "ax"),
        check_vma=False,
    )
```
